512 devices in a mesh: dp: 64 (over y, z), cluster: 8 (over x, core).
Axes of the slice: x: 4, y: 8, z: 8, core: 2. Of those that a mesh axis runs over, the one named last changes fastest.
Arguments:
- embeddings: bfloat16 [32768, 1024], P('dp'), may hold values from -1 to 1, as said below
- centroids: bfloat16 [4096, 1024], P('cluster'), may hold values from -1 to 1, as said below
Outputs:
- refreshed_centroids: float32 [4096, 1024], P(('cluster', 'dp'))
- row_scale_logarithm: float32 [32768], P('dp')
- col_log_scale: float32 [4096], P('cluster')
The draws below stay inside these ranges and needn't reach their ends.
Inputs may be any that keep to these rules, and one draw needn't show every extreme that they name: Every row of embeddings and of centroids has unit Euclidean length up to bfloat16 rounding. `centroids`: every row has unit Euclidean length up to bfloat16 rounding.
All inputs are finite; a program needn't handle non-finite values.
Results may differ from the reference program's by a relative error of at most 0.0014.
Values sent between devices are 32-bit elements; how exact they have to be, the bound alone decides.
A program may use at most 64 MiB of HBM per device.

```python
import jax
import jax.numpy as jnp

D = 1024
K = 4096
ITERS = 3
TOKENS = 32768


def unit_rows(matrix):
    return matrix / jnp.sqrt(jnp.sum(matrix * matrix, axis=1, keepdims=True))


def centers(key):
    return unit_rows(jax.random.normal(key, (K, D), jnp.float32))


def popular_picks(key):
    draws = jax.random.randint(key, (TOKENS,), 0, K)
    return draws * draws // K * draws // K


def draw_centroids(key, part):
    base = centers(key)
    key = jax.random.fold_in(key, 1)
    jitter = jax.random.normal(key, (K, D), jnp.float32) * (0.5 / D ** 0.5)
    return unit_rows(base + jitter).astype(jnp.bfloat16)


def draw_embeddings(key, part):
    base = centers(key)
    key = jax.random.fold_in(key, 2)
    picks = popular_picks(jax.random.fold_in(key, 1))
    noise = jax.random.normal(jax.random.fold_in(key, 2), (TOKENS, D), jnp.float32)
    mixing = 0.95
    rows = mixing * base[picks] + (1.0 - mixing * mixing) ** 0.5 * noise / D ** 0.5
    return unit_rows(rows).astype(jnp.bfloat16)


def setup_inputs(seed: int = 0) -> dict:
    keys = jax.random.split(jax.random.key(seed), 3)
    embeddings = draw_embeddings(jax.random.fold_in(keys[2], 71), 0)
    centroids = draw_centroids(jax.random.fold_in(keys[2], 71), 0)
    return dict(embeddings=embeddings, centroids=centroids)


SOFTMAX_TEMP = 0.1


def reference(embeddings, centroids):
    assignment_logits = jnp.dot(embeddings, centroids.T, preferred_element_type=jnp.float32)
    affinity_scores = jnp.exp(assignment_logits / SOFTMAX_TEMP)
    row_scale_factor = jnp.ones((TOKENS,), jnp.float32)
    col_scale = jnp.ones((K,), jnp.float32)
    for sweep in range(ITERS):
        col_scale = (TOKENS / K) / jnp.sum(affinity_scores * row_scale_factor[:, None], axis=0)
        row_scale_factor = 1.0 / jnp.sum(affinity_scores * col_scale[None, :], axis=1)
    plan = row_scale_factor[:, None] * affinity_scores * col_scale[None, :]
    mass = jnp.sum(plan, axis=0)
    numerators = jnp.dot(plan.astype(jnp.bfloat16).T, embeddings, preferred_element_type=jnp.float32)
    return numerators / mass[:, None], jnp.log(row_scale_factor), jnp.log(col_scale)
```

```python
import functools

import jax
import jax.numpy as jnp
from jax import lax
from jax.experimental import pallas as pl
from jax.experimental.pallas import tpu as pltpu
from jax.sharding import PartitionSpec as P

ITERS = 3
INV_TEMP = 10.0
RATIO = 8.0
NY, NZ, NCL = 8, 8, 8
N, K, D = 512, 512, 1024
LANES = 128
T = N // LANES
HALF = D // 2
MESH = pl.DeviceIdType.MESH


def ring_dist(a, n=8):
    return min(a, n - a)


DP_OFFSETS = sorted(
    ((a, b) for a in range(NY) for b in range(NZ) if a or b),
    key=lambda p: -(ring_dist(p[0]) + ring_dist(p[1])),
)
RING_OFFSETS = (4, 3, 5, 2, 6, 1, 7)
CL_OFFSETS = (4, 5, 3, 2, 6, 7, 1)


def transposed_sum(p):
    return jnp.sum(p.T, axis=0, keepdims=True)


def weighted_sums(m_ref, v, put):
    for j in range(T):
        rows = slice(j * LANES, (j + 1) * LANES)
        p = m_ref[rows, 0:LANES] * v[0:1, :]
        for q in range(1, T):
            p += m_ref[rows, q * LANES : (q + 1) * LANES] * v[q : q + 1, :]
        put(j, transposed_sum(p))


def main_kernel(
    e_hbm, c_hbm, out_ref, r_ref, c_ref,
    e_ref, cent_ref, s_ref, st_ref, plan_ref, num_a, num_b, red_a, red_b,
    col_send, col_recv, row_send, row_recv, mass_send, mass_recv,
    got_a, got_b, fin_a, fin_b,
    load_sem, col_ssem, col_rsem, row_ssem, row_rsem, mass_sems, a_sems, b_sems, fa_sems, fb_sems,
):
    dp = lax.axis_index("dp")
    cl = lax.axis_index("cluster")
    y, z = dp // NZ, lax.rem(dp, NZ)

    def dp_dev(dy, dz):
        return lax.rem(y + dy, NY) * NZ + lax.rem(z + dz, NZ)

    load_e = pltpu.make_async_copy(e_hbm, e_ref, load_sem.at[0])
    load_c = pltpu.make_async_copy(c_hbm, cent_ref, load_sem.at[1])
    load_e.start()
    load_c.start()

    barrier = pltpu.get_barrier_semaphore()
    for dy, dz in DP_OFFSETS:
        pl.semaphore_signal(barrier, inc=1, device_id=(dp_dev(dy, dz), cl), device_id_type=MESH)
    for j in CL_OFFSETS:
        pl.semaphore_signal(barrier, inc=1, device_id=(dp, lax.rem(cl + j, NCL)), device_id_type=MESH)

    load_e.wait()
    load_c.wait()
    nt = (((1,), (1,)), ((), ()))
    for j in range(T):
        rows = slice(j * LANES, (j + 1) * LANES)
        st_ref[rows, :] = jnp.exp(
            lax.dot_general(cent_ref[rows, :], e_ref[...], nt, preferred_element_type=jnp.float32) * INV_TEMP
        )
    for j in range(T):
        rows = slice(j * LANES, (j + 1) * LANES)
        s_ref[rows, :] = jnp.exp(
            lax.dot_general(e_ref[rows, :], cent_ref[...], nt, preferred_element_type=jnp.float32) * INV_TEMP
        )
    pl.semaphore_wait(barrier, len(DP_OFFSETS) + len(CL_OFFSETS))

    def total_wait(buf, sem):
        pltpu.make_async_copy(buf, buf, sem).wait()

    def iteration(it, r):
        def put_col(j, v):
            col_send[it, j : j + 1, :] = v

        weighted_sums(st_ref, r, put_col)
        for i, (dy, dz) in enumerate(DP_OFFSETS):
            pltpu.make_async_remote_copy(
                col_send.at[it], col_recv.at[it, i], col_ssem.at[it], col_rsem.at[it],
                device_id=(dp_dev(dy, dz), cl), device_id_type=MESH,
            ).start()
        total_wait(col_recv.at[it], col_rsem.at[it])
        c = RATIO / (col_send[it] + jnp.sum(col_recv[it], axis=0))
        c_ref[...] = c

        def put_row(j, v):
            row_send[it, j : j + 1, :] = v

        weighted_sums(s_ref, c, put_row)
        for i, j in enumerate(CL_OFFSETS):
            pltpu.make_async_remote_copy(
                row_send.at[it], row_recv.at[it, i], row_ssem.at[it], row_rsem.at[it],
                device_id=(dp, lax.rem(cl + j, NCL)), device_id_type=MESH,
            ).start()

        @pl.when(it == ITERS - 1)
        def _():
            for j in range(T):
                rows = slice(j * LANES, (j + 1) * LANES)
                c_col = jnp.broadcast_to(c[j : j + 1, :], (LANES, LANES)).T
                for q in range(T):
                    cols = slice(q * LANES, (q + 1) * LANES)
                    st_ref[rows, cols] = st_ref[rows, cols] * c_col

        total_wait(row_recv.at[it], row_rsem.at[it])
        return 1.0 / (row_send[it] + jnp.sum(row_recv[it], axis=0))

    r = lax.fori_loop(0, ITERS, iteration, jnp.ones((T, LANES), jnp.float32))
    r_ref[...] = r

    for j in range(T):
        rows = slice(j * LANES, (j + 1) * LANES)
        p = None
        for q in range(T):
            cols = slice(q * LANES, (q + 1) * LANES)
            plan = st_ref[rows, cols] * r[q : q + 1, :]
            p = plan if p is None else p + plan
            plan_ref[rows, cols] = plan.astype(jnp.bfloat16)
        mass_send[j] = transposed_sum(p)

    num_a[...] = jnp.dot(
        plan_ref[...], e_ref[:, :HALF], preferred_element_type=jnp.float32
    ).reshape(NY, NZ, 8, HALF)
    for dy in RING_OFFSETS:
        pltpu.make_async_remote_copy(
            num_a.at[lax.rem(y + dy, NY)], got_a.at[dy - 1], a_sems.at[0], a_sems.at[1],
            device_id=(dp_dev(dy, 0), cl), device_id_type=MESH,
        ).start()
    num_b[...] = jnp.dot(
        plan_ref[...], e_ref[:, HALF:], preferred_element_type=jnp.float32
    ).reshape(NY, NZ, 8, HALF)
    for dz in RING_OFFSETS:
        pltpu.make_async_remote_copy(
            num_b.at[:, lax.rem(z + dz, NZ)], got_b.at[dz - 1], b_sems.at[0], b_sems.at[1],
            device_id=(dp_dev(0, dz), cl), device_id_type=MESH,
        ).start()
    for i, (dy, dz) in enumerate(DP_OFFSETS):
        owner = dp_dev(dy, dz)
        pltpu.make_async_remote_copy(
            mass_send.at[owner // (LANES // 8)], mass_recv.at[i], mass_sems.at[0], mass_sems.at[1],
            device_id=(owner, cl), device_id_type=MESH,
        ).start()

    total_wait(got_a, a_sems.at[1])
    for k in range(8):
        red_a[k] = num_a[y, k] + jnp.sum(got_a[:, k], axis=0)
    for dz in RING_OFFSETS:
        pltpu.make_async_remote_copy(
            red_a.at[lax.rem(z + dz, NZ)], fin_a.at[dz - 1], fa_sems.at[0], fa_sems.at[1],
            device_id=(dp_dev(0, dz), cl), device_id_type=MESH,
        ).start()
    total_wait(got_b, b_sems.at[1])
    for k in range(8):
        red_b[k] = num_b[k, z] + jnp.sum(got_b[:, k], axis=0)
    for dy in RING_OFFSETS:
        pltpu.make_async_remote_copy(
            red_b.at[lax.rem(y + dy, NY)], fin_b.at[dy - 1], fb_sems.at[0], fb_sems.at[1],
            device_id=(dp_dev(dy, 0), cl), device_id_type=MESH,
        ).start()

    total_wait(mass_recv, mass_sems.at[1])
    mass_row = mass_send[dp // (LANES // 8)] + jnp.sum(mass_recv[...], axis=0)
    mine = lax.broadcasted_iota(jnp.int32, (8, LANES), 1) == (
        lax.rem(dp, LANES // 8) * 8 + lax.broadcasted_iota(jnp.int32, (8, LANES), 0)
    )
    mass = jnp.sum(jnp.where(mine, jnp.broadcast_to(mass_row, (8, LANES)), 0.0), axis=1, keepdims=True)

    total_wait(fin_a, fa_sems.at[1])
    out_ref[:, :HALF] = (red_a[z] + jnp.sum(fin_a[...], axis=0)) / mass
    total_wait(fin_b, fb_sems.at[1])
    out_ref[:, HALF:] = (red_b[y] + jnp.sum(fin_b[...], axis=0)) / mass

    for it in range(ITERS):
        total_wait(col_recv.at[it], col_ssem.at[it])
        total_wait(row_recv.at[it], row_ssem.at[it])
    total_wait(got_a, a_sems.at[0])
    total_wait(got_b, b_sems.at[0])
    total_wait(mass_recv, mass_sems.at[0])
    total_wait(fin_a, fa_sems.at[0])
    total_wait(fin_b, fb_sems.at[0])


def finish_kernel(num_ref, r_ref, c_ref, out_ref, lr_ref, lc_ref):
    out_ref[...] = num_ref[...]
    lr_ref[...] = jnp.log(r_ref[...])
    lc_ref[...] = jnp.log(c_ref[...])


def per_device(embeddings, centroids):
    f32 = jnp.float32
    vmem = pl.BlockSpec(memory_space=pltpu.VMEM)
    hbm = pl.BlockSpec(memory_space=pl.ANY)
    dma = pltpu.SemaphoreType.DMA
    outs = (
        jax.ShapeDtypeStruct((8, D), f32),
        jax.ShapeDtypeStruct((T, LANES), f32),
        jax.ShapeDtypeStruct((T, LANES), f32),
    )
    n_dp, n_cl = len(DP_OFFSETS), len(CL_OFFSETS)
    num, r, c = pl.pallas_call(
        main_kernel,
        out_shape=outs,
        in_specs=[hbm, hbm],
        out_specs=(vmem, vmem, vmem),
        scratch_shapes=[
            pltpu.VMEM((N, D), jnp.bfloat16),
            pltpu.VMEM((K, D), jnp.bfloat16),
            pltpu.VMEM((N, K), f32),
            pltpu.VMEM((K, N), f32),
            pltpu.VMEM((K, N), jnp.bfloat16),
            pltpu.VMEM((NY, NZ, 8, HALF), f32),
            pltpu.VMEM((NY, NZ, 8, HALF), f32),
            pltpu.VMEM((NZ, 8, HALF), f32),
            pltpu.VMEM((NY, 8, HALF), f32),
            pltpu.VMEM((ITERS, T, LANES), f32),
            pltpu.VMEM((ITERS, n_dp, T, LANES), f32),
            pltpu.VMEM((ITERS, T, LANES), f32),
            pltpu.VMEM((ITERS, n_cl, T, LANES), f32),
            pltpu.VMEM((T, 1, LANES), f32),
            pltpu.VMEM((n_dp, 1, LANES), f32),
            pltpu.VMEM((NY - 1, NZ, 8, HALF), f32),
            pltpu.VMEM((NZ - 1, NY, 8, HALF), f32),
            pltpu.VMEM((NZ - 1, 8, HALF), f32),
            pltpu.VMEM((NY - 1, 8, HALF), f32),
            dma((2,)),
            dma((ITERS,)),
            dma((ITERS,)),
            dma((ITERS,)),
            dma((ITERS,)),
            dma((2,)),
            dma((2,)),
            dma((2,)),
            dma((2,)),
            dma((2,)),
        ],
        compiler_params=pltpu.CompilerParams(
            collective_id=0, has_side_effects=True, vmem_limit_bytes=48 * 2**20
        ),
    )(embeddings, centroids)
    out, lr, lc = pl.pallas_call(
        finish_kernel, out_shape=outs, in_specs=[vmem] * 3, out_specs=(vmem,) * 3
    )(num, r, c)
    return out, lr.reshape(N), lc.reshape(K)


def solution(mesh):
    in_specs = (P("dp", None), P("cluster", None))
    out_specs = (P(("cluster", "dp"), None), P("dp"), P("cluster"))
    return jax.shard_map(
        per_device, mesh=mesh, in_specs=in_specs, out_specs=out_specs, check_vma=False
    )
```

```python
import functools

import jax
import jax.numpy as jnp
from jax import lax
from jax.experimental import pallas as pl
from jax.experimental.pallas import tpu as pltpu
from jax.sharding import PartitionSpec as P

ITERS = 3
INV_TEMP = 10.0
RATIO = 8.0
NY, NZ, NCL = 8, 8, 8
N, K, D = 512, 512, 1024
LANES = 128
T = N // LANES
HALF = D // 2
CHUNKS = 2
W = HALF // CHUNKS
STEPS = 4
VMEM_LIMIT = 63 * 2**20
MESH = pl.DeviceIdType.MESH


def ring_dist(a, n=8):
    return min(a, n - a)


DP_OFFSETS = sorted(
    ((a, b) for a in range(NY) for b in range(NZ) if a or b),
    key=lambda p: -(ring_dist(p[0]) + ring_dist(p[1])),
)
RING_OFFSETS = (4, 3, 5, 2, 6, 1, 7)
CL_OFFSETS = (4, 5, 3, 2, 6, 7, 1)


def transposed_sum(p):
    return jnp.sum(p.T, axis=0, keepdims=True)


def weighted_sums(m_ref, v, put):
    for j in range(T):
        rows = slice(j * LANES, (j + 1) * LANES)
        p = m_ref[rows, 0:LANES] * v[0:1, :]
        for q in range(1, T):
            p += m_ref[rows, q * LANES : (q + 1) * LANES] * v[q : q + 1, :]
        put(j, transposed_sum(p))


def main_kernel(
    e_hbm, c_hbm, out_ref,
    e_ref, cent_ref, s_ref, st_ref, plan_ref, num, got, red, fin,
    col_send, col_recv, row_send, row_recv, mass_send, mass_recv,
    load_sem, col_ssem, col_rsem, row_ssem, row_rsem, mass_sems, ring_ssem, ring_rsem, fin_ssem, fin_rsem,
):
    dp = lax.axis_index("dp")
    cl = lax.axis_index("cluster")
    y, z = dp // NZ, lax.rem(dp, NZ)

    def dp_dev(dy, dz):
        return lax.rem(y + dy, NY) * NZ + lax.rem(z + dz, NZ)

    load_e = pltpu.make_async_copy(e_hbm, e_ref, load_sem.at[0])
    load_c = pltpu.make_async_copy(c_hbm, cent_ref, load_sem.at[1])
    load_e.start()
    load_c.start()

    barrier = pltpu.get_barrier_semaphore()
    for dy, dz in DP_OFFSETS:
        pl.semaphore_signal(barrier, inc=1, device_id=(dp_dev(dy, dz), cl), device_id_type=MESH)
    for j in CL_OFFSETS:
        pl.semaphore_signal(barrier, inc=1, device_id=(dp, lax.rem(cl + j, NCL)), device_id_type=MESH)

    load_e.wait()
    load_c.wait()
    nt = (((1,), (1,)), ((), ()))

    def score_rows(j, _):
        rows = pl.ds(pl.multiple_of(j * LANES, LANES), LANES)
        st_ref[rows, :] = jnp.exp(
            lax.dot_general(cent_ref[rows, :], e_ref[...], nt, preferred_element_type=jnp.float32) * INV_TEMP
        )
        s_ref[rows, :] = jnp.exp(
            lax.dot_general(e_ref[rows, :], cent_ref[...], nt, preferred_element_type=jnp.float32) * INV_TEMP
        )
        return 0

    lax.fori_loop(0, T, score_rows, 0)
    pl.semaphore_wait(barrier, len(DP_OFFSETS) + len(CL_OFFSETS))

    def total_wait(buf, sem):
        pltpu.make_async_copy(buf, buf, sem).wait()

    def iteration(it, r):
        def put_col(j, v):
            col_send[it, j : j + 1, :] = v

        weighted_sums(st_ref, r, put_col)
        for i, (dy, dz) in enumerate(DP_OFFSETS):
            pltpu.make_async_remote_copy(
                col_send.at[it], col_recv.at[it, i], col_ssem.at[it], col_rsem.at[it],
                device_id=(dp_dev(dy, dz), cl), device_id_type=MESH,
            ).start()
        total_wait(col_recv.at[it], col_rsem.at[it])
        c = RATIO / (col_send[it] + jnp.sum(col_recv[it], axis=0))
        out_ref[NZ, T : 2 * T, :] = c

        def put_row(j, v):
            row_send[it, j : j + 1, :] = v

        weighted_sums(s_ref, c, put_row)
        for i, j in enumerate(CL_OFFSETS):
            pltpu.make_async_remote_copy(
                row_send.at[it], row_recv.at[it, i], row_ssem.at[it], row_rsem.at[it],
                device_id=(dp, lax.rem(cl + j, NCL)), device_id_type=MESH,
            ).start()

        @pl.when(it == ITERS - 1)
        def _():
            for j in range(T):
                rows = slice(j * LANES, (j + 1) * LANES)
                c_col = jnp.broadcast_to(c[j : j + 1, :], (LANES, LANES)).T
                for q in range(T):
                    cols = slice(q * LANES, (q + 1) * LANES)
                    st_ref[rows, cols] = st_ref[rows, cols] * c_col

        total_wait(row_recv.at[it], row_rsem.at[it])
        return 1.0 / (row_send[it] + jnp.sum(row_recv[it], axis=0))

    r = lax.fori_loop(0, ITERS, iteration, jnp.ones((T, LANES), jnp.float32))
    out_ref[NZ, 0:T, :] = r

    for j in range(T):
        rows = slice(j * LANES, (j + 1) * LANES)
        p = None
        for q in range(T):
            cols = slice(q * LANES, (q + 1) * LANES)
            plan = st_ref[rows, cols] * r[q : q + 1, :]
            p = plan if p is None else p + plan
            plan_ref[rows, cols] = plan.astype(jnp.bfloat16)
        mass_send[j] = transposed_sum(p)

    for i, (dy, dz) in enumerate(DP_OFFSETS):
        owner = dp_dev(dy, dz)
        pltpu.make_async_remote_copy(
            mass_send.at[owner // (LANES // 8)], mass_recv.at[i], mass_sems.at[0], mass_sems.at[1],
            device_id=(owner, cl), device_id_type=MESH,
        ).start()

    place = (y, z)
    other = (z, y)

    def device_at(h, step, along):
        shift = (step, 0) if (h == 0) == along else (0, step)
        return (dp_dev(*shift), cl)

    def ring_send(h, ch, way, s):
        if s == 1:
            owner = lax.rem(place[h] + 4, 8)
            part = pl.ds(4 * way, 4)
        else:
            owner = lax.rem(place[h] + (3 + s if way == 0 else 5 - s), 8)
            part = pl.ds(0, 8)
        pltpu.make_async_remote_copy(
            num.at[h, ch, owner, part], got.at[h, way, ch, s - 1, part],
            ring_ssem.at[h, way, ch], ring_rsem.at[h, way, ch, s - 1],
            device_id=device_at(h, 7 if way == 0 else 1, True), device_id_type=MESH,
        ).start()

    def ring_take(h, ch, way, s):
        part = pl.ds(4 * way, 4) if s == 1 else pl.ds(0, 8)
        total_wait(got.at[h, way, ch, s - 1, part], ring_rsem.at[h, way, ch, s - 1])
        owner = lax.rem(place[h] + (4 + s if way == 0 else 4 - s), 8)
        num[h, ch, owner, part] += got[h, way, ch, s - 1, part]

    for ch in range(CHUNKS):
        for h in range(2):
            cols = slice(h * HALF + ch * W, h * HALF + (ch + 1) * W)
            block = jnp.dot(plan_ref[...], e_ref[:, cols], preferred_element_type=jnp.float32).reshape(8, 8, 8, W)
            if h == 0:
                num[h, ch] = block
            else:
                for k in range(8):
                    num[h, ch, :, k] = block[k]
            for way in range(2):
                ring_send(h, ch, way, 1)
    for s in range(1, STEPS):
        for ch in range(CHUNKS):
            for h in range(2):
                for way in range(2):
                    ring_take(h, ch, way, s)
                    ring_send(h, ch, way, s + 1)
    for ch in range(CHUNKS):
        for h in range(2):
            for way in range(2):
                ring_take(h, ch, way, STEPS)
            red[h, ch] = num[h, ch, place[h]]
            for d in RING_OFFSETS:
                pltpu.make_async_remote_copy(
                    red.at[h, ch, lax.rem(other[h] + d, 8)], fin.at[h, ch, d - 1], fin_ssem.at[h, ch], fin_rsem.at[h, ch],
                    device_id=device_at(h, d, False), device_id_type=MESH,
                ).start()

    total_wait(mass_recv, mass_sems.at[1])
    mass_row = mass_send[dp // (LANES // 8)] + jnp.sum(mass_recv[...], axis=0)
    mine = lax.broadcasted_iota(jnp.int32, (8, LANES), 1) == (
        lax.rem(dp, LANES // 8) * 8 + lax.broadcasted_iota(jnp.int32, (8, LANES), 0)
    )
    mass = jnp.sum(jnp.where(mine, jnp.broadcast_to(mass_row, (8, LANES)), 0.0), axis=1, keepdims=True)
    for ch in range(CHUNKS):
        for h in range(2):
            total_wait(fin.at[h, ch], fin_rsem.at[h, ch])
            block = (red[h, ch, other[h]] + jnp.sum(fin[h, ch], axis=0)) / mass
            for q in range(W // LANES):
                out_ref[(h * HALF + ch * W) // LANES + q] = block[:, q * LANES : (q + 1) * LANES]

    for it in range(ITERS):
        total_wait(col_recv.at[it], col_ssem.at[it])
        total_wait(row_recv.at[it], row_ssem.at[it])
    total_wait(mass_recv, mass_sems.at[0])
    for h in range(2):
        for ch in range(CHUNKS):
            total_wait(fin.at[h, ch], fin_ssem.at[h, ch])
            for way in range(2):
                total_wait(got.at[h, way, ch, pl.ds(0, 3)], ring_ssem.at[h, way, ch])
                total_wait(got.at[h, way, ch, 3, pl.ds(0, 4)], ring_ssem.at[h, way, ch])


def finish_kernel(all_ref, out_ref, lr_ref, lc_ref):
    for j in range(D // LANES):
        out_ref[:, j * LANES : (j + 1) * LANES] = all_ref[j]
    lr_ref[...] = jnp.log(all_ref[NZ, 0:T, :])
    lc_ref[...] = jnp.log(all_ref[NZ, T : 2 * T, :])


def per_device(embeddings, centroids):
    f32 = jnp.float32
    vmem = pl.BlockSpec(memory_space=pltpu.VMEM)
    hbm = pl.BlockSpec(memory_space=pl.ANY)
    dma = pltpu.SemaphoreType.DMA
    outs = (
        jax.ShapeDtypeStruct((8, D), f32),
        jax.ShapeDtypeStruct((T, LANES), f32),
        jax.ShapeDtypeStruct((T, LANES), f32),
    )
    n_dp, n_cl = len(DP_OFFSETS), len(CL_OFFSETS)
    packed = pl.pallas_call(
        main_kernel,
        out_shape=jax.ShapeDtypeStruct((D // LANES + 1, 8, LANES), f32),
        in_specs=[hbm, hbm],
        out_specs=vmem,
        scratch_shapes=[
            pltpu.VMEM((N, D), jnp.bfloat16),
            pltpu.VMEM((K, D), jnp.bfloat16),
            pltpu.VMEM((N, K), f32),
            pltpu.VMEM((K, N), f32),
            pltpu.VMEM((K, N), jnp.bfloat16),
            pltpu.VMEM((2, CHUNKS, 8, 8, 8, W), f32),
            pltpu.VMEM((2, 2, CHUNKS, STEPS, 8, 8, W), f32),
            pltpu.VMEM((2, CHUNKS, 8, 8, W), f32),
            pltpu.VMEM((2, CHUNKS, 7, 8, W), f32),
            pltpu.VMEM((ITERS, T, LANES), f32),
            pltpu.VMEM((ITERS, n_dp, T, LANES), f32),
            pltpu.VMEM((ITERS, T, LANES), f32),
            pltpu.VMEM((ITERS, n_cl, T, LANES), f32),
            pltpu.VMEM((T, 1, LANES), f32),
            pltpu.VMEM((n_dp, 1, LANES), f32),
            dma((2,)),
            dma((ITERS,)),
            dma((ITERS,)),
            dma((ITERS,)),
            dma((ITERS,)),
            dma((2,)),
            dma((2, 2, CHUNKS)),
            dma((2, 2, CHUNKS, STEPS)),
            dma((2, CHUNKS)),
            dma((2, CHUNKS)),
        ],
        compiler_params=pltpu.CompilerParams(
            collective_id=0, has_side_effects=True, vmem_limit_bytes=VMEM_LIMIT
        ),
    )(embeddings, centroids)
    out, lr, lc = pl.pallas_call(
        finish_kernel, out_shape=outs, in_specs=[vmem], out_specs=(vmem,) * 3,
        compiler_params=pltpu.CompilerParams(vmem_limit_bytes=2**20),
    )(packed)
    return out, lr.reshape(N), lc.reshape(K)


def solution(mesh):
    in_specs = (P("dp", None), P("cluster", None))
    out_specs = (P(("cluster", "dp"), None), P("dp"), P("cluster"))
    return jax.shard_map(
        per_device, mesh=mesh, in_specs=in_specs, out_specs=out_specs, check_vma=False
    )
```

```python
import functools

import jax
import jax.numpy as jnp
from jax import lax
from jax.experimental import pallas as pl
from jax.experimental.pallas import tpu as pltpu
from jax.sharding import PartitionSpec as P

ITERS = 3
INV_TEMP = 10.0
RATIO = 8.0
NY, NZ, NCL = 8, 8, 8
N, K, D = 512, 512, 1024
LANES = 128
T = N // LANES
HALF = D // 2
CHUNKS = 4
W = HALF // CHUNKS
SLOTS = 4
VMEM_LIMIT = 267 * 2**20 // 5
MESH = pl.DeviceIdType.MESH


def ring_dist(a, n=8):
    return min(a, n - a)


DP_OFFSETS = sorted(
    ((a, b) for a in range(NY) for b in range(NZ) if a or b),
    key=lambda p: -(ring_dist(p[0]) + ring_dist(p[1])),
)
RING_OFFSETS = (4, 3, 5, 2, 6, 1, 7)
CL_OFFSETS = (4, 5, 3, 2, 6, 7, 1)


def transposed_sum(p):
    return jnp.sum(p.T, axis=0, keepdims=True)


def weighted_sums(m_ref, v, put):
    for j in range(T):
        rows = slice(j * LANES, (j + 1) * LANES)
        p = m_ref[rows, 0:LANES] * v[0:1, :]
        for q in range(1, T):
            p += m_ref[rows, q * LANES : (q + 1) * LANES] * v[q : q + 1, :]
        put(j, transposed_sum(p))


def main_kernel(
    e_hbm, c_hbm, out_ref,
    e_ref, cent_ref, s_ref, st_ref, plan_ref, num, got, red, fin,
    col_send, col_recv, row_send, row_recv, mass_send, mass_recv,
    load_sem, col_ssem, col_rsem, row_ssem, row_rsem, mass_sems, ring_ssem, ring_rsem, fin_ssem, fin_rsem,
):
    dp = lax.axis_index("dp")
    cl = lax.axis_index("cluster")
    y, z = dp // NZ, lax.rem(dp, NZ)

    def dp_dev(dy, dz):
        return lax.rem(y + dy, NY) * NZ + lax.rem(z + dz, NZ)

    load_e = pltpu.make_async_copy(e_hbm, e_ref, load_sem.at[0])
    load_c = pltpu.make_async_copy(c_hbm, cent_ref, load_sem.at[1])
    load_e.start()
    load_c.start()

    barrier = pltpu.get_barrier_semaphore()
    for dy, dz in DP_OFFSETS:
        pl.semaphore_signal(barrier, inc=1, device_id=(dp_dev(dy, dz), cl), device_id_type=MESH)
    for j in CL_OFFSETS:
        pl.semaphore_signal(barrier, inc=1, device_id=(dp, lax.rem(cl + j, NCL)), device_id_type=MESH)

    load_e.wait()
    load_c.wait()
    nt = (((1,), (1,)), ((), ()))

    def score_rows(j, _):
        rows = pl.ds(pl.multiple_of(j * LANES, LANES), LANES)
        st_ref[rows, :] = jnp.exp(
            lax.dot_general(cent_ref[rows, :], e_ref[...], nt, preferred_element_type=jnp.float32) * INV_TEMP
        )
        s_ref[rows, :] = jnp.exp(
            lax.dot_general(e_ref[rows, :], cent_ref[...], nt, preferred_element_type=jnp.float32) * INV_TEMP
        )
        return 0

    lax.fori_loop(0, T, score_rows, 0)
    pl.semaphore_wait(barrier, len(DP_OFFSETS) + len(CL_OFFSETS))

    def total_wait(buf, sem):
        pltpu.make_async_copy(buf, buf, sem).wait()

    def iteration(it, r):
        def put_col(j, v):
            col_send[it, j : j + 1, :] = v

        weighted_sums(st_ref, r, put_col)
        for i, (dy, dz) in enumerate(DP_OFFSETS):
            pltpu.make_async_remote_copy(
                col_send.at[it], col_recv.at[it, i], col_ssem.at[it], col_rsem.at[it],
                device_id=(dp_dev(dy, dz), cl), device_id_type=MESH,
            ).start()
        total_wait(col_recv.at[it], col_rsem.at[it])
        c = RATIO / (col_send[it] + jnp.sum(col_recv[it], axis=0))
        out_ref[NZ, T : 2 * T, :] = c

        def put_row(j, v):
            row_send[it, j : j + 1, :] = v

        weighted_sums(s_ref, c, put_row)
        for i, j in enumerate(CL_OFFSETS):
            pltpu.make_async_remote_copy(
                row_send.at[it], row_recv.at[it, i], row_ssem.at[it], row_rsem.at[it],
                device_id=(dp, lax.rem(cl + j, NCL)), device_id_type=MESH,
            ).start()

        @pl.when(it == ITERS - 1)
        def _():
            for j in range(T):
                rows = slice(j * LANES, (j + 1) * LANES)
                c_col = jnp.broadcast_to(c[j : j + 1, :], (LANES, LANES)).T
                for q in range(T):
                    cols = slice(q * LANES, (q + 1) * LANES)
                    st_ref[rows, cols] = st_ref[rows, cols] * c_col

        total_wait(row_recv.at[it], row_rsem.at[it])
        return 1.0 / (row_send[it] + jnp.sum(row_recv[it], axis=0))

    r = lax.fori_loop(0, ITERS, iteration, jnp.ones((T, LANES), jnp.float32))
    out_ref[NZ, 0:T, :] = r

    for j in range(T):
        rows = slice(j * LANES, (j + 1) * LANES)
        p = None
        for q in range(T):
            cols = slice(q * LANES, (q + 1) * LANES)
            plan = st_ref[rows, cols] * r[q : q + 1, :]
            p = plan if p is None else p + plan
            plan_ref[rows, cols] = plan.astype(jnp.bfloat16)
        mass_send[j] = transposed_sum(p)

    place = (y, z)
    other = (z, y)

    def device_at(h, step, along):
        shift = (step, 0) if (h == 0) == along else (0, step)
        return (dp_dev(*shift), cl)

    def ring_part(way, slot):
        return pl.ds(4 * way, 4) if slot == 0 else pl.ds(0, 8)

    def ring_owner(h, way, distance):
        return lax.rem(place[h] + (8 - distance if way == 0 else distance), 8)

    def ring_send(h, ch, way, slot):
        hops = 2 if slot == 0 else 1
        owner, part = ring_owner(h, way, 4 - slot), ring_part(way, slot)
        pltpu.make_async_remote_copy(
            num.at[h, ch, owner, part], got.at[h, way, ch, slot, part],
            ring_ssem.at[h, way, ch], ring_rsem.at[h, way, ch, slot],
            device_id=device_at(h, 8 - hops if way == 0 else hops, True), device_id_type=MESH,
        ).start()

    def ring_take(h, ch, way, slot):
        part = ring_part(way, slot)
        total_wait(got.at[h, way, ch, slot, part], ring_rsem.at[h, way, ch, slot])
        num[h, ch, ring_owner(h, way, min(2, 3 - slot)), part] += got[h, way, ch, slot, part]

    for ch in range(CHUNKS):
        for h in range(2):
            cols = slice(h * HALF + ch * W, h * HALF + (ch + 1) * W)
            block = jnp.dot(plan_ref[...], e_ref[:, cols], preferred_element_type=jnp.float32).reshape(8, 8, 8, W)
            if h == 0:
                num[h, ch] = block
            else:
                for k in range(8):
                    num[h, ch, :, k] = block[k]
            for slot in range(2):
                for way in range(2):
                    ring_send(h, ch, way, slot)
    for i, (dy, dz) in enumerate(DP_OFFSETS):
        owner = dp_dev(dy, dz)
        pltpu.make_async_remote_copy(
            mass_send.at[owner // (LANES // 8)], mass_recv.at[i], mass_sems.at[0], mass_sems.at[1],
            device_id=(owner, cl), device_id_type=MESH,
        ).start()

    for slot in (2, 3):
        for ch in range(CHUNKS):
            for h in range(2):
                for way in range(2):
                    if slot == 2:
                        ring_take(h, ch, way, 0)
                    ring_take(h, ch, way, slot - 1)
                    ring_send(h, ch, way, slot)
    for ch in range(CHUNKS):
        for h in range(2):
            for way in range(2):
                ring_take(h, ch, way, 3)
            red[h, ch] = num[h, ch, place[h]]
            for d in RING_OFFSETS:
                pltpu.make_async_remote_copy(
                    red.at[h, ch, lax.rem(other[h] + d, 8)], fin.at[h, ch, d - 1], fin_ssem.at[h, ch], fin_rsem.at[h, ch],
                    device_id=device_at(h, d, False), device_id_type=MESH,
                ).start()

    total_wait(mass_recv, mass_sems.at[1])
    mass_row = mass_send[dp // (LANES // 8)] + jnp.sum(mass_recv[...], axis=0)
    mine = lax.broadcasted_iota(jnp.int32, (8, LANES), 1) == (
        lax.rem(dp, LANES // 8) * 8 + lax.broadcasted_iota(jnp.int32, (8, LANES), 0)
    )
    mass = jnp.sum(jnp.where(mine, jnp.broadcast_to(mass_row, (8, LANES)), 0.0), axis=1, keepdims=True)
    for ch in range(CHUNKS):
        for h in range(2):
            total_wait(fin.at[h, ch], fin_rsem.at[h, ch])
            block = (red[h, ch, other[h]] + jnp.sum(fin[h, ch], axis=0)) / mass
            for q in range(W // LANES):
                out_ref[(h * HALF + ch * W) // LANES + q] = block[:, q * LANES : (q + 1) * LANES]

    for it in range(ITERS):
        total_wait(col_recv.at[it], col_ssem.at[it])
        total_wait(row_recv.at[it], row_ssem.at[it])
    total_wait(mass_recv, mass_sems.at[0])
    for h in range(2):
        for ch in range(CHUNKS):
            total_wait(fin.at[h, ch], fin_ssem.at[h, ch])
            for way in range(2):
                total_wait(got.at[h, way, ch, pl.ds(0, 3)], ring_ssem.at[h, way, ch])
                total_wait(got.at[h, way, ch, 3, pl.ds(0, 4)], ring_ssem.at[h, way, ch])


def finish_kernel(all_ref, out_ref, lr_ref, lc_ref):
    for j in range(D // LANES):
        out_ref[:, j * LANES : (j + 1) * LANES] = all_ref[j]
    lr_ref[...] = jnp.log(all_ref[NZ, 0:T, :])
    lc_ref[...] = jnp.log(all_ref[NZ, T : 2 * T, :])


def per_device(embeddings, centroids):
    f32 = jnp.float32
    vmem = pl.BlockSpec(memory_space=pltpu.VMEM)
    hbm = pl.BlockSpec(memory_space=pl.ANY)
    dma = pltpu.SemaphoreType.DMA
    outs = (
        jax.ShapeDtypeStruct((8, D), f32),
        jax.ShapeDtypeStruct((T, LANES), f32),
        jax.ShapeDtypeStruct((T, LANES), f32),
    )
    n_dp, n_cl = len(DP_OFFSETS), len(CL_OFFSETS)
    packed = pl.pallas_call(
        main_kernel,
        out_shape=jax.ShapeDtypeStruct((D // LANES + 1, 8, LANES), f32),
        in_specs=[hbm, hbm],
        out_specs=vmem,
        scratch_shapes=[
            pltpu.VMEM((N, D), jnp.bfloat16),
            pltpu.VMEM((K, D), jnp.bfloat16),
            pltpu.VMEM((N, K), f32),
            pltpu.VMEM((K, N), f32),
            pltpu.VMEM((K, N), jnp.bfloat16),
            pltpu.VMEM((2, CHUNKS, 8, 8, 8, W), f32),
            pltpu.VMEM((2, 2, CHUNKS, SLOTS, 8, 8, W), f32),
            pltpu.VMEM((2, CHUNKS, 8, 8, W), f32),
            pltpu.VMEM((2, CHUNKS, 7, 8, W), f32),
            pltpu.VMEM((ITERS, T, LANES), f32),
            pltpu.VMEM((ITERS, n_dp, T, LANES), f32),
            pltpu.VMEM((ITERS, T, LANES), f32),
            pltpu.VMEM((ITERS, n_cl, T, LANES), f32),
            pltpu.VMEM((T, 1, LANES), f32),
            pltpu.VMEM((n_dp, 1, LANES), f32),
            dma((2,)),
            dma((ITERS,)),
            dma((ITERS,)),
            dma((ITERS,)),
            dma((ITERS,)),
            dma((2,)),
            dma((2, 2, CHUNKS)),
            dma((2, 2, CHUNKS, SLOTS)),
            dma((2, CHUNKS)),
            dma((2, CHUNKS)),
        ],
        compiler_params=pltpu.CompilerParams(
            collective_id=0, has_side_effects=True, vmem_limit_bytes=VMEM_LIMIT
        ),
    )(embeddings, centroids)
    out, lr, lc = pl.pallas_call(
        finish_kernel, out_shape=outs, in_specs=[vmem], out_specs=(vmem,) * 3,
        compiler_params=pltpu.CompilerParams(vmem_limit_bytes=2**20),
    )(packed)
    return out, lr.reshape(N), lc.reshape(K)


def solution(mesh):
    in_specs = (P("dp", None), P("cluster", None))
    out_specs = (P(("cluster", "dp"), None), P("dp"), P("cluster"))
    return jax.shard_map(
        per_device, mesh=mesh, in_specs=in_specs, out_specs=out_specs, check_vma=False
    )
```

```python
import functools

import jax
import jax.numpy as jnp
from jax import lax
from jax.experimental import pallas as pl
from jax.experimental.pallas import tpu as pltpu
from jax.sharding import PartitionSpec as P

ITERS = 3
INV_TEMP = 10.0
RATIO = 8.0
NY, NZ, NCL = 8, 8, 8
N, K, D = 512, 512, 1024
LANES = 128
T = N // LANES
HALF = D // 2
CHUNKS = 4
W = HALF // CHUNKS
SLOTS = 4
GROUP = 2
GROUPS = CHUNKS // GROUP
VMEM_LIMIT = 267 * 2**20 // 5
MESH = pl.DeviceIdType.MESH


def ring_dist(a, n=8):
    return min(a, n - a)


DP_OFFSETS = sorted(
    ((a, b) for a in range(NY) for b in range(NZ) if a or b),
    key=lambda p: -(ring_dist(p[0]) + ring_dist(p[1])),
)
RING_OFFSETS = (4, 3, 5, 2, 6, 1, 7)
CL_OFFSETS = (4, 5, 3, 2, 6, 7, 1)


def transposed_sum(p):
    return jnp.sum(p.T, axis=0, keepdims=True)


def weighted_sums(m_ref, v, put):
    for j in range(T):
        rows = slice(j * LANES, (j + 1) * LANES)
        p = m_ref[rows, 0:LANES] * v[0:1, :]
        for q in range(1, T):
            p += m_ref[rows, q * LANES : (q + 1) * LANES] * v[q : q + 1, :]
        put(j, transposed_sum(p))


def main_kernel(
    e_hbm, c_hbm, out_ref,
    e_ref, cent_ref, s_ref, st_ref, plan_ref, num, got, red, fin,
    col_send, col_recv, row_send, row_recv, mass_send, mass_part, mass_recv,
    load_sem, col_ssem, col_rsem, row_ssem, row_rsem, mass_sems, ring_ssem, ring_rsem, fin_ssem, fin_rsem,
):
    dp = lax.axis_index("dp")
    cl = lax.axis_index("cluster")
    y, z = dp // NZ, lax.rem(dp, NZ)

    row_start = [lax.rem(y + d, NY) * NZ for d in range(NY)]
    in_row = [lax.rem(z + d, NZ) for d in range(NZ)]

    def dp_dev(dy, dz):
        return row_start[dy] + in_row[dz]

    load_e = pltpu.make_async_copy(e_hbm, e_ref, load_sem.at[0])
    load_c = pltpu.make_async_copy(c_hbm, cent_ref, load_sem.at[1])
    load_e.start()
    load_c.start()

    barrier = pltpu.get_barrier_semaphore()
    for dy, dz in DP_OFFSETS:
        pl.semaphore_signal(barrier, inc=1, device_id=(dp_dev(dy, dz), cl), device_id_type=MESH)
    for j in CL_OFFSETS:
        pl.semaphore_signal(barrier, inc=1, device_id=(dp, lax.rem(cl + j, NCL)), device_id_type=MESH)

    load_e.wait()
    load_c.wait()
    nt = (((1,), (1,)), ((), ()))

    def scores(left, right, to):
        def block(j, _):
            rows = pl.ds(pl.multiple_of(j * LANES, LANES), LANES)
            to[rows, :] = jnp.exp(
                lax.dot_general(left[rows, :], right[...], nt, preferred_element_type=jnp.float32) * INV_TEMP
            )
            return 0

        lax.fori_loop(0, T, block, 0)

    scores(cent_ref, e_ref, st_ref)

    def total_wait(buf, sem):
        pltpu.make_async_copy(buf, buf, sem).wait()

    def column_sums(it, r):
        def put_col(j, v):
            col_send[it, j : j + 1, :] = v

        weighted_sums(st_ref, r, put_col)

    column_sums(0, jnp.ones((T, LANES), jnp.float32))
    pl.semaphore_wait(barrier, len(DP_OFFSETS) + len(CL_OFFSETS))

    def iteration(it):
        for i, (dy, dz) in enumerate(DP_OFFSETS):
            pltpu.make_async_remote_copy(
                col_send.at[it], col_recv.at[it, i], col_ssem.at[it], col_rsem.at[it],
                device_id=(dp_dev(dy, dz), cl), device_id_type=MESH,
            ).start()
        if it == 0:
            scores(e_ref, cent_ref, s_ref)
        total_wait(col_recv.at[it], col_rsem.at[it])
        c = RATIO / (col_send[it] + jnp.sum(col_recv[it], axis=0))
        out_ref[NZ, T : 2 * T, :] = c

        def put_row(j, v):
            row_send[it, j : j + 1, :] = v

        weighted_sums(s_ref, c, put_row)
        for i, j in enumerate(CL_OFFSETS):
            pltpu.make_async_remote_copy(
                row_send.at[it], row_recv.at[it, i], row_ssem.at[it], row_rsem.at[it],
                device_id=(dp, lax.rem(cl + j, NCL)), device_id_type=MESH,
            ).start()

        if it == ITERS - 1:
            for j in range(T):
                rows = slice(j * LANES, (j + 1) * LANES)
                c_col = jnp.broadcast_to(c[j : j + 1, :], (LANES, LANES)).T
                for q in range(T):
                    cols = slice(q * LANES, (q + 1) * LANES)
                    st_ref[rows, cols] = st_ref[rows, cols] * c_col

        total_wait(row_recv.at[it], row_rsem.at[it])
        r = 1.0 / (row_send[it] + jnp.sum(row_recv[it], axis=0))

        if it < ITERS - 1:
            column_sums(it + 1, r)
        return r

    for it in range(ITERS):
        r = iteration(it)
    out_ref[NZ, 0:T, :] = r

    for j in range(T):
        rows = slice(j * LANES, (j + 1) * LANES)
        p = None
        for q in range(T):
            cols = slice(q * LANES, (q + 1) * LANES)
            plan = st_ref[rows, cols] * r[q : q + 1, :]
            p = plan if p is None else p + plan
            plan_ref[rows, cols] = plan.astype(jnp.bfloat16)
        mass_send[j] = transposed_sum(p)

    place = (y, z)
    other = (z, y)

    def device_at(h, step, along):
        shift = (step, 0) if (h == 0) == along else (0, step)
        return (dp_dev(*shift), cl)

    def ring_part(way, slot):
        return pl.ds(4 * way, 4) if slot == 0 else pl.ds(0, 8)

    def ring_owner(h, way, distance):
        return lax.rem(place[h] + (8 - distance if way == 0 else distance), 8)

    def ring_send(h, ch, way, slot):
        hops = 2 if slot == 0 else 1
        owner, part = ring_owner(h, way, 4 - slot), ring_part(way, slot)
        pltpu.make_async_remote_copy(
            num.at[h, ch, owner, part], got.at[h, way, ch, slot, part],
            ring_ssem.at[h, way], ring_rsem.at[h, way, ch, slot],
            device_id=device_at(h, 8 - hops if way == 0 else hops, True), device_id_type=MESH,
        ).start()

    def ring_take(h, ch, way, slot):
        part = ring_part(way, slot)
        total_wait(got.at[h, way, ch, slot, part], ring_rsem.at[h, way, ch, slot])
        num[h, ch, ring_owner(h, way, min(2, 3 - slot)), part] += got[h, way, ch, slot, part]

    for g in range(GROUPS):
        for h in range(2):
            first = h * HALF + g * GROUP * W
            block = jnp.dot(
                plan_ref[...], e_ref[:, first : first + GROUP * W], preferred_element_type=jnp.float32
            ).reshape(8, 8, 8, GROUP * W)
            for i in range(GROUP):
                ch, part = g * GROUP + i, block[..., i * W : (i + 1) * W]
                if h == 0:
                    num[h, ch] = part
                else:
                    for k in range(8):
                        num[h, ch, :, k] = part[k]
                for slot in range(2):
                    for way in range(2):
                        ring_send(h, ch, way, slot)
    for d in RING_OFFSETS:
        owner = dp_dev(d, 0)
        pltpu.make_async_remote_copy(
            mass_send.at[owner // (LANES // 8)], mass_recv.at[0, d - 1], mass_sems.at[0], mass_sems.at[1],
            device_id=(owner, cl), device_id_type=MESH,
        ).start()
    for slot in (2, 3):
        for ch in range(CHUNKS):
            for h in range(2):
                for way in range(2):
                    if slot == 2:
                        ring_take(h, ch, way, 0)
                    ring_take(h, ch, way, slot - 1)
                    ring_send(h, ch, way, slot)
    total_wait(mass_recv.at[0], mass_sems.at[1])
    mass_part[...] = mass_send[dp // (LANES // 8)] + jnp.sum(mass_recv[0], axis=0)
    for d in RING_OFFSETS:
        pltpu.make_async_remote_copy(
            mass_part, mass_recv.at[1, d - 1], mass_sems.at[2], mass_sems.at[3],
            device_id=(dp_dev(0, d), cl), device_id_type=MESH,
        ).start()
    for g in range(GROUPS):
        for h in range(2):
            for i in range(GROUP):
                ch = g * GROUP + i
                for way in range(2):
                    total_wait(got.at[h, way, ch, 3], ring_rsem.at[h, way, ch, 3])
                red[h, g, :, i] = num[h, ch, place[h]] + got[h, 0, ch, 3] + got[h, 1, ch, 3]
            for d in RING_OFFSETS:
                pltpu.make_async_remote_copy(
                    red.at[h, g, lax.rem(other[h] + d, 8)], fin.at[h, g, d - 1], fin_ssem.at[h], fin_rsem.at[h, g],
                    device_id=device_at(h, d, False), device_id_type=MESH,
                ).start()

    for it in range(ITERS):
        total_wait(col_recv.at[it], col_ssem.at[it])
        total_wait(row_recv.at[it], row_ssem.at[it])
    total_wait(mass_recv.at[0], mass_sems.at[0])
    for h in range(2):
        for way in range(2):
            total_wait(got.at[h, way, :, pl.ds(0, 3)], ring_ssem.at[h, way])
            total_wait(got.at[h, way, :, 3, pl.ds(0, 4)], ring_ssem.at[h, way])

    total_wait(mass_recv.at[1], mass_sems.at[3])
    total_wait(mass_recv.at[1], mass_sems.at[2])
    mass_row = mass_part[...] + jnp.sum(mass_recv[1], axis=0)
    mine = lax.broadcasted_iota(jnp.int32, (8, LANES), 1) == (
        lax.rem(dp, LANES // 8) * 8 + lax.broadcasted_iota(jnp.int32, (8, LANES), 0)
    )
    mass = jnp.sum(jnp.where(mine, jnp.broadcast_to(mass_row, (8, LANES)), 0.0), axis=1, keepdims=True)
    for g in range(GROUPS):
        for h in range(2):
            total_wait(fin.at[h, g], fin_rsem.at[h, g])
            for i in range(GROUP):
                block = (red[h, g, other[h], i] + jnp.sum(fin[h, g, :, i], axis=0)) / mass
                for q in range(W // LANES):
                    out_ref[(h * HALF + (g * GROUP + i) * W) // LANES + q] = block[:, q * LANES : (q + 1) * LANES]
    for h in range(2):
        total_wait(fin.at[h], fin_ssem.at[h])


def finish_kernel(all_ref, out_ref, lr_ref, lc_ref):
    for j in range(D // LANES):
        out_ref[:, j * LANES : (j + 1) * LANES] = all_ref[j]
    lr_ref[...] = jnp.log(all_ref[NZ, 0:T, :])
    lc_ref[...] = jnp.log(all_ref[NZ, T : 2 * T, :])


def per_device(embeddings, centroids):
    f32 = jnp.float32
    vmem = pl.BlockSpec(memory_space=pltpu.VMEM)
    hbm = pl.BlockSpec(memory_space=pl.ANY)
    dma = pltpu.SemaphoreType.DMA
    outs = (
        jax.ShapeDtypeStruct((8, D), f32),
        jax.ShapeDtypeStruct((T, LANES), f32),
        jax.ShapeDtypeStruct((T, LANES), f32),
    )
    n_dp, n_cl = len(DP_OFFSETS), len(CL_OFFSETS)
    packed = pl.pallas_call(
        main_kernel,
        out_shape=jax.ShapeDtypeStruct((D // LANES + 1, 8, LANES), f32),
        in_specs=[hbm, hbm],
        out_specs=vmem,
        scratch_shapes=[
            pltpu.VMEM((N, D), jnp.bfloat16),
            pltpu.VMEM((K, D), jnp.bfloat16),
            pltpu.VMEM((N, K), f32),
            pltpu.VMEM((K, N), f32),
            pltpu.VMEM((K, N), jnp.bfloat16),
            pltpu.VMEM((2, CHUNKS, 8, 8, 8, W), f32),
            pltpu.VMEM((2, 2, CHUNKS, SLOTS, 8, 8, W), f32),
            pltpu.VMEM((2, GROUPS, 8, GROUP, 8, W), f32),
            pltpu.VMEM((2, GROUPS, 7, GROUP, 8, W), f32),
            pltpu.VMEM((ITERS, T, LANES), f32),
            pltpu.VMEM((ITERS, n_dp, T, LANES), f32),
            pltpu.VMEM((ITERS, T, LANES), f32),
            pltpu.VMEM((ITERS, n_cl, T, LANES), f32),
            pltpu.VMEM((T, 1, LANES), f32),
            pltpu.VMEM((1, LANES), f32),
            pltpu.VMEM((2, 7, 1, LANES), f32),
            dma((2,)),
            dma((ITERS,)),
            dma((ITERS,)),
            dma((ITERS,)),
            dma((ITERS,)),
            dma((4,)),
            dma((2, 2)),
            dma((2, 2, CHUNKS, SLOTS)),
            dma((2,)),
            dma((2, GROUPS)),
        ],
        compiler_params=pltpu.CompilerParams(
            collective_id=0, has_side_effects=True, vmem_limit_bytes=VMEM_LIMIT
        ),
    )(embeddings, centroids)
    out, lr, lc = pl.pallas_call(
        finish_kernel, out_shape=outs, in_specs=[vmem], out_specs=(vmem,) * 3,
        compiler_params=pltpu.CompilerParams(vmem_limit_bytes=2**20),
    )(packed)
    return out, lr.reshape(N), lc.reshape(K)


def solution(mesh):
    in_specs = (P("dp", None), P("cluster", None))
    out_specs = (P(("cluster", "dp"), None), P("dp"), P("cluster"))
    return jax.shard_map(
        per_device, mesh=mesh, in_specs=in_specs, out_specs=out_specs, check_vma=False
    )
```

```python
import functools

import jax
import jax.numpy as jnp
from jax import lax
from jax.experimental import pallas as pl
from jax.experimental.pallas import tpu as pltpu
from jax.sharding import PartitionSpec as P

ITERS = 3
INV_TEMP = 10.0
RATIO = 8.0
NY, NZ, NCL = 8, 8, 8
N, K, D = 512, 512, 1024
LANES = 128
T = N // LANES
HALF = D // 2
CHUNKS = 4
W = HALF // CHUNKS
SLOTS = 4
GROUP = 2
GROUPS = CHUNKS // GROUP
VMEM_LIMIT = 267 * 2**20 // 5
MESH = pl.DeviceIdType.MESH


def ring_dist(a, n=8):
    return min(a, n - a)


DP_OFFSETS = sorted(
    ((a, b) for a in range(NY) for b in range(NZ) if a or b),
    key=lambda p: -(ring_dist(p[0]) + ring_dist(p[1])),
)
RING_OFFSETS = (4, 3, 5, 2, 6, 1, 7)
CL_OFFSETS = (4, 5, 3, 2, 6, 7, 1)


def transposed_sum(p):
    return jnp.sum(p.T, axis=0, keepdims=True)


def weighted_sums(m_ref, v, put):
    for j in range(T):
        rows = slice(j * LANES, (j + 1) * LANES)
        p = m_ref[rows, 0:LANES] * v[0:1, :]
        for q in range(1, T):
            p += m_ref[rows, q * LANES : (q + 1) * LANES] * v[q : q + 1, :]
        put(j, transposed_sum(p))


def main_kernel(
    e_hbm, c_hbm, out_ref,
    e_ref, cent_ref, s_ref, st_ref, plan_ref, num, got, red, fin,
    col_send, col_recv, row_send, row_recv, mass_send, mass_part, mass_recv,
    load_sem, col_ssem, col_rsem, row_ssem, row_rsem, mass_sems, ring_ssem, ring_rsem, fin_ssem, fin_rsem,
):
    dp = lax.axis_index("dp")
    cl = lax.axis_index("cluster")
    y, z = dp // NZ, lax.rem(dp, NZ)

    row_start = [lax.rem(y + d, NY) * NZ for d in range(NY)]
    in_row = [lax.rem(z + d, NZ) for d in range(NZ)]

    def dp_dev(dy, dz):
        return row_start[dy] + in_row[dz]

    load_e = pltpu.make_async_copy(e_hbm, e_ref, load_sem.at[0])
    load_c = pltpu.make_async_copy(c_hbm, cent_ref, load_sem.at[1])
    load_e.start()
    load_c.start()

    barrier = pltpu.get_barrier_semaphore()
    for dy, dz in DP_OFFSETS:
        pl.semaphore_signal(barrier, inc=1, device_id=(dp_dev(dy, dz), cl), device_id_type=MESH)
    for j in CL_OFFSETS:
        pl.semaphore_signal(barrier, inc=1, device_id=(dp, lax.rem(cl + j, NCL)), device_id_type=MESH)

    load_e.wait()
    load_c.wait()
    nt = (((1,), (1,)), ((), ()))

    def scores(left, right, to):
        def block(j, _):
            rows = pl.ds(pl.multiple_of(j * LANES, LANES), LANES)
            to[rows, :] = jnp.exp(
                lax.dot_general(left[rows, :], right[...], nt, preferred_element_type=jnp.float32) * INV_TEMP
            )
            return 0

        lax.fori_loop(0, T, block, 0)

    scores(cent_ref, e_ref, st_ref)

    def total_wait(buf, sem):
        pltpu.make_async_copy(buf, buf, sem).wait()

    def column_sums(it, r):
        def put_col(j, v):
            col_send[it, j : j + 1, :] = v

        weighted_sums(st_ref, r, put_col)

    column_sums(0, jnp.ones((T, LANES), jnp.float32))
    pl.semaphore_wait(barrier, len(DP_OFFSETS) + len(CL_OFFSETS))

    def iteration(it):
        for i, (dy, dz) in enumerate(DP_OFFSETS):
            pltpu.make_async_remote_copy(
                col_send.at[it], col_recv.at[it, i], col_ssem.at[it], col_rsem.at[it],
                device_id=(dp_dev(dy, dz), cl), device_id_type=MESH,
            ).start()
        if it == 0:
            scores(e_ref, cent_ref, s_ref)
        total_wait(col_recv.at[it], col_rsem.at[it])
        c = RATIO / (col_send[it] + jnp.sum(col_recv[it], axis=0))
        out_ref[NZ, T : 2 * T, :] = c

        def put_row(j, v):
            row_send[it, j : j + 1, :] = v

        weighted_sums(s_ref, c, put_row)
        for i, j in enumerate(CL_OFFSETS):
            pltpu.make_async_remote_copy(
                row_send.at[it], row_recv.at[it, i], row_ssem.at[it], row_rsem.at[it],
                device_id=(dp, lax.rem(cl + j, NCL)), device_id_type=MESH,
            ).start()

        if it == ITERS - 1:
            for j in range(T):
                rows = slice(j * LANES, (j + 1) * LANES)
                c_col = jnp.broadcast_to(c[j : j + 1, :], (LANES, LANES)).T
                for q in range(T):
                    cols = slice(q * LANES, (q + 1) * LANES)
                    st_ref[rows, cols] = st_ref[rows, cols] * c_col

        total_wait(row_recv.at[it], row_rsem.at[it])
        r = 1.0 / (row_send[it] + jnp.sum(row_recv[it], axis=0))

        if it < ITERS - 1:
            column_sums(it + 1, r)
        return r

    for it in range(ITERS):
        r = iteration(it)
    out_ref[NZ, 0:T, :] = r

    for j in range(T):
        rows = slice(j * LANES, (j + 1) * LANES)
        p = None
        for q in range(T):
            cols = slice(q * LANES, (q + 1) * LANES)
            plan = st_ref[rows, cols] * r[q : q + 1, :]
            p = plan if p is None else p + plan
            plan_ref[rows, cols] = plan.astype(jnp.bfloat16)
        mass_send[j] = transposed_sum(p)

    place = (y, z)
    other = (z, y)

    def device_at(h, step, along):
        shift = (step, 0) if (h == 0) == along else (0, step)
        return (dp_dev(*shift), cl)

    def ring_owner(h, way, distance):
        return lax.rem(place[h] + (8 - distance if way == 0 else distance), 8)

    def ring_send(h, ch, way, slot):
        hops = 2 if slot == 0 else 1
        owner = ring_owner(h, way, 4 - slot)
        pltpu.make_async_remote_copy(
            num.at[h, ch, owner], got.at[h, way, ch, slot],
            ring_ssem.at[h, way], ring_rsem.at[h, way, ch, slot],
            device_id=device_at(h, 8 - hops if way == 0 else hops, True), device_id_type=MESH,
        ).start()

    def ring_take(h, ch, way, slot):
        total_wait(got.at[h, way, ch, slot], ring_rsem.at[h, way, ch, slot])
        num[h, ch, ring_owner(h, way, min(2, 3 - slot))] += got[h, way, ch, slot]

    for g in range(GROUPS):
        for h in range(2):
            first = h * HALF + g * GROUP * W
            block = jnp.dot(
                plan_ref[...], e_ref[:, first : first + GROUP * W], preferred_element_type=jnp.float32
            ).reshape(8, 8, 8, GROUP * W)
            for i in range(GROUP):
                ch, part = g * GROUP + i, block[..., i * W : (i + 1) * W]
                if h == 0:
                    num[h, ch] = part
                else:
                    for k in range(8):
                        num[h, ch, :, k] = part[k]
                for slot in range(2):
                    for way in range(2):
                        if slot or way == ch % 2:
                            ring_send(h, ch, way, slot)
    for d in RING_OFFSETS:
        owner = dp_dev(d, 0)
        pltpu.make_async_remote_copy(
            mass_send.at[owner // (LANES // 8)], mass_recv.at[0, d - 1], mass_sems.at[0], mass_sems.at[1],
            device_id=(owner, cl), device_id_type=MESH,
        ).start()
    for slot in (2, 3):
        for ch in range(CHUNKS):
            for h in range(2):
                for way in range(2):
                    if slot == 2 and way == ch % 2:
                        ring_take(h, ch, way, 0)
                    ring_take(h, ch, way, slot - 1)
                    ring_send(h, ch, way, slot)
    total_wait(mass_recv.at[0], mass_sems.at[1])
    mass_part[...] = mass_send[dp // (LANES // 8)] + jnp.sum(mass_recv[0], axis=0)
    for d in RING_OFFSETS:
        pltpu.make_async_remote_copy(
            mass_part, mass_recv.at[1, d - 1], mass_sems.at[2], mass_sems.at[3],
            device_id=(dp_dev(0, d), cl), device_id_type=MESH,
        ).start()
    for g in range(GROUPS):
        for h in range(2):
            for i in range(GROUP):
                ch = g * GROUP + i
                for way in range(2):
                    total_wait(got.at[h, way, ch, 3], ring_rsem.at[h, way, ch, 3])
                red[h, g, :, i] = num[h, ch, place[h]] + got[h, 0, ch, 3] + got[h, 1, ch, 3]
            for d in RING_OFFSETS:
                pltpu.make_async_remote_copy(
                    red.at[h, g, lax.rem(other[h] + d, 8)], fin.at[h, g, d - 1], fin_ssem.at[h], fin_rsem.at[h, g],
                    device_id=device_at(h, d, False), device_id_type=MESH,
                ).start()

    for it in range(ITERS):
        total_wait(col_recv.at[it], col_ssem.at[it])
        total_wait(row_recv.at[it], row_ssem.at[it])
    total_wait(mass_recv.at[0], mass_sems.at[0])
    for h in range(2):
        for way in range(2):
            total_wait(got.at[h, way, :, pl.ds(0, 3)], ring_ssem.at[h, way])
            total_wait(got.at[h, way, pl.ds(0, CHUNKS // 2), 3], ring_ssem.at[h, way])

    total_wait(mass_recv.at[1], mass_sems.at[3])
    total_wait(mass_recv.at[1], mass_sems.at[2])
    mass_row = mass_part[...] + jnp.sum(mass_recv[1], axis=0)
    mine = lax.broadcasted_iota(jnp.int32, (8, LANES), 1) == (
        lax.rem(dp, LANES // 8) * 8 + lax.broadcasted_iota(jnp.int32, (8, LANES), 0)
    )
    mass = jnp.sum(jnp.where(mine, jnp.broadcast_to(mass_row, (8, LANES)), 0.0), axis=1, keepdims=True)
    for g in range(GROUPS):
        for h in range(2):
            total_wait(fin.at[h, g], fin_rsem.at[h, g])
            for i in range(GROUP):
                block = (red[h, g, other[h], i] + jnp.sum(fin[h, g, :, i], axis=0)) / mass
                for q in range(W // LANES):
                    out_ref[(h * HALF + (g * GROUP + i) * W) // LANES + q] = block[:, q * LANES : (q + 1) * LANES]
    for h in range(2):
        total_wait(fin.at[h], fin_ssem.at[h])


def finish_kernel(all_ref, out_ref, lr_ref, lc_ref):
    for j in range(D // LANES):
        out_ref[:, j * LANES : (j + 1) * LANES] = all_ref[j]
    lr_ref[...] = jnp.log(all_ref[NZ, 0:T, :])
    lc_ref[...] = jnp.log(all_ref[NZ, T : 2 * T, :])


def per_device(embeddings, centroids):
    f32 = jnp.float32
    vmem = pl.BlockSpec(memory_space=pltpu.VMEM)
    hbm = pl.BlockSpec(memory_space=pl.ANY)
    dma = pltpu.SemaphoreType.DMA
    outs = (
        jax.ShapeDtypeStruct((8, D), f32),
        jax.ShapeDtypeStruct((T, LANES), f32),
        jax.ShapeDtypeStruct((T, LANES), f32),
    )
    n_dp, n_cl = len(DP_OFFSETS), len(CL_OFFSETS)
    packed = pl.pallas_call(
        main_kernel,
        out_shape=jax.ShapeDtypeStruct((D // LANES + 1, 8, LANES), f32),
        in_specs=[hbm, hbm],
        out_specs=vmem,
        scratch_shapes=[
            pltpu.VMEM((N, D), jnp.bfloat16),
            pltpu.VMEM((K, D), jnp.bfloat16),
            pltpu.VMEM((N, K), f32),
            pltpu.VMEM((K, N), f32),
            pltpu.VMEM((K, N), jnp.bfloat16),
            pltpu.VMEM((2, CHUNKS, 8, 8, 8, W), f32),
            pltpu.VMEM((2, 2, CHUNKS, SLOTS, 8, 8, W), f32),
            pltpu.VMEM((2, GROUPS, 8, GROUP, 8, W), f32),
            pltpu.VMEM((2, GROUPS, 7, GROUP, 8, W), f32),
            pltpu.VMEM((ITERS, T, LANES), f32),
            pltpu.VMEM((ITERS, n_dp, T, LANES), f32),
            pltpu.VMEM((ITERS, T, LANES), f32),
            pltpu.VMEM((ITERS, n_cl, T, LANES), f32),
            pltpu.VMEM((T, 1, LANES), f32),
            pltpu.VMEM((1, LANES), f32),
            pltpu.VMEM((2, 7, 1, LANES), f32),
            dma((2,)),
            dma((ITERS,)),
            dma((ITERS,)),
            dma((ITERS,)),
            dma((ITERS,)),
            dma((4,)),
            dma((2, 2)),
            dma((2, 2, CHUNKS, SLOTS)),
            dma((2,)),
            dma((2, GROUPS)),
        ],
        compiler_params=pltpu.CompilerParams(
            collective_id=0, has_side_effects=True, vmem_limit_bytes=VMEM_LIMIT
        ),
    )(embeddings, centroids)
    out, lr, lc = pl.pallas_call(
        finish_kernel, out_shape=outs, in_specs=[vmem], out_specs=(vmem,) * 3,
        compiler_params=pltpu.CompilerParams(vmem_limit_bytes=2**20),
    )(packed)
    return out, lr.reshape(N), lc.reshape(K)


def solution(mesh):
    in_specs = (P("dp", None), P("cluster", None))
    out_specs = (P(("cluster", "dp"), None), P("dp"), P("cluster"))
    return jax.shard_map(
        per_device, mesh=mesh, in_specs=in_specs, out_specs=out_specs, check_vma=False
    )
```
